128 devices in a mesh: blk: 8 (over x_lo, y), grp: 16 (over z, x_hi, core).
Axes of the slice: x: 4 (x_hi: 2, x_lo: 2; x = x_hi * 2 + x_lo), y: 4, z: 4, core: 2. Of those that a mesh axis runs over, the one named last changes fastest.
Arguments:
- picture_vectors: bfloat16 [16384, 1152], P(('blk', 'grp')), may hold values from -1.1953125 to 1.1953125
- caption_vectors: bfloat16 [16384, 1152], P(('blk', 'grp')), may hold values from -1.1953125 to 1.1953125
- matching_caption: int32 [16384], P(('blk', 'grp')), may hold values from 0 to 16383, each once
- sharpness_parameter: float32 [1], replicated, may hold values from 1 to 4
- additive_intercept: float32 [1], replicated, may hold values from -6 to -2
Outputs:
- picture_derivative: float32 [16384, 1152], P(('blk', 'grp'))
- text_grad: float32 [16384, 1152], P(('blk', 'grp'))
The draws below stay inside these ranges and needn't reach their ends.
Inputs may be any that keep to these rules, and one draw needn't show every extreme that they name: matching_caption is a permutation: each text is the positive of exactly one image.
All inputs are finite; a program needn't handle non-finite values.
Results may differ from the reference program's by a relative error of at most 0.0011.
Values may be sent and summed in bfloat16 or wider, within the bound.
A program may use at most 64 MiB of HBM per device.

```python
import math
import jax
import jax.numpy as jnp
from jax import lax

D = 1152
BATCH = 16384


def block_levels(rng, shape, cuts, smallest, top_value):
    gain = 1.0
    for axis_at, parts in cuts:
        steps = jax.random.uniform(jax.random.fold_in(jax.random.fold_in(rng, 6), axis_at), (parts,), jnp.float32, smallest / len(cuts), top_value / len(cuts))
        gain = gain * jnp.repeat(jnp.exp(steps), shape[axis_at] // parts).reshape((-1,) + (1,) * (len(shape) - 1 - axis_at))
    return gain


def bell_draw(key, dims, scale, bound, cuts=(), held_as=jnp.bfloat16):
    drawn = jax.random.normal(key, dims, jnp.float32) * scale
    if len(cuts) > 0:
        drawn = block_levels(key, dims, cuts, -0.22, 0.18) * drawn
    return jnp.clip(drawn, min=-bound, max=bound).astype(held_as)


def setup_inputs(seed: int = 0) -> dict:
    splits = jax.random.split(jax.random.key(seed), 6)
    return {
        "picture_vectors": bell_draw(splits[0], (BATCH, D), 0.2, 1.1953125, ((0, 128),)),
        "caption_vectors": bell_draw(splits[1], (BATCH, D), 0.2, 1.1953125, ((0, 128),)),
        "matching_caption": jax.random.permutation(splits[2], BATCH).astype(jnp.int32),
        "sharpness_parameter": jnp.clip(jnp.exp(jax.random.uniform(splits[3], (1,), jnp.float32, math.log(1.0), math.log(4.0))), 1.0, 4.0),
        "additive_intercept": jnp.clip(jax.random.uniform(splits[4], (1,), jnp.float32, -6.0, -2.0), -6.0, -2.0),
    }


def piece_derivative(pinned_sample, guest_captions, matching_pair, sharpness_factor, moved_intercept):
    similarity_matrix = jnp.dot(pinned_sample, guest_captions.T, preferred_element_type=jnp.float32)
    pair_coefficients = (jax.nn.sigmoid(sharpness_factor * similarity_matrix + moved_intercept) - matching_pair).astype(jnp.bfloat16)
    return sharpness_factor * jnp.dot(pair_coefficients, guest_captions, preferred_element_type=jnp.float32)


def reference(picture_vectors, caption_vectors, matching_caption, sharpness_parameter, additive_intercept):
    sharpness_factor = sharpness_parameter[0]
    moved_intercept = additive_intercept[0]
    row_block = BATCH // 8
    all_ids = jnp.arange(BATCH, dtype=jnp.int32)

    def image_rows(start):
        pinned_sample = lax.dynamic_slice_in_dim(picture_vectors, start, row_block, 0)
        own_pairs = lax.dynamic_slice_in_dim(matching_caption, start, row_block, 0)
        matching_pair = (own_pairs[:, None] == all_ids[None, :]).astype(jnp.float32)
        return piece_derivative(pinned_sample, caption_vectors, matching_pair, sharpness_factor, moved_intercept)

    def text_rows(start):
        pinned_sample = lax.dynamic_slice_in_dim(caption_vectors, start, row_block, 0)
        own_ids = start + jnp.arange(row_block, dtype=jnp.int32)
        matching_pair = (own_ids[:, None] == matching_caption[None, :]).astype(jnp.float32)
        return piece_derivative(pinned_sample, picture_vectors, matching_pair, sharpness_factor, moved_intercept)

    starts = jnp.arange(8, dtype=jnp.int32) * row_block
    picture_derivative = lax.map(image_rows, starts).reshape(BATCH, -1)
    text_grad = lax.map(text_rows, starts).reshape(BATCH, -1)
    return picture_derivative, text_grad
```

```python
import functools

import jax
import jax.numpy as jnp
from jax import lax
from jax.experimental import pallas as pl
from jax.experimental.pallas import tpu as pltpu
from jax.sharding import PartitionSpec as P

MESH = pl.DeviceIdType.MESH
ORDER = [(0, 0), (3, 0), (1, 0), (2, 0), (0, 1), (3, 1), (1, 1), (2, 1)]
SLOT = {key: i for i, key in enumerate(ORDER)}
SHARE = 128
HALF = 64
UNIT = 32
MESSAGES = 17
TOP = 32767.0


def peers():
    b, g = lax.axis_index("blk"), lax.axis_index("grp")
    xl, y = b // 4, lax.rem(b, 4)
    z, low = g // 4, lax.rem(g, 4)
    xh, core = low // 2, lax.rem(low, 2)

    def at(xl, y, z, xh, core):
        return (xl * 4 + y, z * 4 + xh * 2 + core)

    up = lambda v: lax.rem(v + 1, 4)
    down = lambda v: lax.rem(v + 3, 4)
    pictures = (at(xl, y, up(z), xh, core), at(xl, y, down(z), xh, core), at(1 - xl, y, z, xh, core))
    captions = (at(xl, up(y), z, xh, core), at(xl, down(y), z, xh, core), at(1 - xl, y, z, 1 - xh, core))
    sibling = at(xl, y, z, xh, 1 - core)
    starts = []
    for dy, dx in ORDER:
        txl = 1 - xl if dx else xl
        txh = 1 - xh if dx else xh
        blk, grp = at(txl, lax.rem(y + dy, 4), z, txh, core)
        starts.append((blk * 16 + grp) * SHARE)
    return pictures, captions, sibling, starts


class Family:
    def __init__(self, shares, step, sums, other, devices, out, first):
        self.shares, self.step, self.sums, self.other = shares, step, sums, other
        self.plus, self.minus, self.pair = devices
        self.out, self.message = out, first
        self.sent = {}

    def rows(self, key, lo, hi):
        return self.shares.at[pl.ds(SLOT[key] * self.step + lo, hi - lo)]


def kernel(
    sharp_ref, shift_ref, picture_ref, caption_ref, label_ref, picture_out, caption_out,
    pictures, captions, labels, weights, picture_sums, caption_sums, sibling_sums,
    out_data, in_data, out_scale, in_scale, local_sem, send_sem, recv_sem,
):
    picture_peers, caption_peers, sibling, starts = peers()
    loads = [
        pltpu.make_async_copy(picture_ref, pictures.at[pl.ds(0, SHARE)], local_sem.at[0]),
        pltpu.make_async_copy(caption_ref, captions.at[pl.ds(0, SHARE)], local_sem.at[1]),
    ]
    for load in loads:
        load.start()
    barrier = pltpu.get_barrier_semaphore()
    everyone = [*picture_peers, *caption_peers, sibling]
    for device in everyone:
        pl.semaphore_signal(barrier, inc=1, device_id=device, device_id_type=MESH)
    labels[0] = jnp.broadcast_to(label_ref[...], (8, SHARE))
    half_sharp = sharp_ref[0] * 0.5
    half_shift = shift_ref[0] * 0.5
    for load in loads:
        load.wait()
    pl.semaphore_wait(barrier, len(everyone))

    copies = []

    def send(src, dst, device):
        i = len(copies)
        copy = pltpu.make_async_remote_copy(
            src_ref=src, dst_ref=dst, send_sem=send_sem.at[i], recv_sem=recv_sem.at[i],
            device_id=device, device_id_type=MESH,
        )
        copy.start()
        copies.append(copy)
        return copy

    images = Family(pictures, 2 * SHARE, picture_sums, sibling_sums, picture_peers, picture_out, 0)
    texts = Family(captions, SHARE, caption_sums, None, caption_peers, caption_out, MESSAGES)
    both = (images, texts)
    mid_p, mid_q = HALF // 2, HALF + HALF // 2

    def hop(f, name, key, lo, hi, to, device):
        f.sent[name] = send(f.rows(key, lo, hi), f.rows(to, lo, hi), device)

    def to_sibling(*keys):
        for key in keys:
            start = SLOT[key] * 2 * SHARE
            images.sent["s", key] = send(
                pictures.at[pl.ds(start, SHARE)], pictures.at[pl.ds(start + SHARE, SHARE)], sibling
            )

    def arrive(f, *names):
        for name in names:
            f.sent[name].wait_recv()

    for f in both:
        hop(f, "q+", (0, 0), HALF, SHARE, (3, 0), f.plus)
        hop(f, "q-", (0, 0), HALF, SHARE, (1, 0), f.minus)
        hop(f, "xp", (0, 0), 0, HALF, (0, 1), f.pair)
    to_sibling((0, 0))

    def label_copy(first, to, count, device):
        return send(labels.at[pl.ds(first, count)], labels.at[pl.ds(to, count)], device)

    label_copy(0, 1, 1, sibling).wait_recv()
    for f in both:
        hop(f, "p+", (0, 0), 0, HALF, (3, 0), f.plus)
        hop(f, "p-", (0, 0), 0, HALF, (1, 0), f.minus)
        hop(f, "xq", (0, 0), HALF, SHARE, (0, 1), f.pair)
    label_copy(0, 2 * SLOT[0, 1], 2, images.pair).wait_recv()
    rounds = []
    for dx in (0, 1):
        mine, above, below = (2 * SLOT[d, dx] for d in (0, 1, 3))
        rounds.append(label_copy(mine, below, 2, images.plus))
        rounds.append(label_copy(mine, above, 2, images.minus))
    for copy in rounds:
        copy.wait_recv()
    rounds = []
    for dx in (0, 1):
        below, across = 2 * SLOT[3, dx], 2 * SLOT[2, dx]
        rounds.append(label_copy(below, across, 2, images.plus))
    for copy in rounds:
        copy.wait_recv()

    for f in both:
        arrive(f, "q+", "q-")
        hop(f, "q++", (3, 0), HALF, mid_q, (2, 0), f.plus)
        hop(f, "q--", (1, 0), mid_q, SHARE, (2, 0), f.minus)
        hop(f, "xq1", (1, 0), HALF, SHARE, (1, 1), f.pair)
        hop(f, "xq3", (3, 0), HALF, SHARE, (3, 1), f.pair)
    for f in both:
        arrive(f, "xp")
        hop(f, "P+", (0, 1), 0, HALF, (3, 1), f.plus)
        hop(f, "P-", (0, 1), 0, HALF, (1, 1), f.minus)
    for f in both:
        arrive(f, "p+", "p-")
        hop(f, "p++", (3, 0), 0, mid_p, (2, 0), f.plus)
        hop(f, "p--", (1, 0), mid_p, HALF, (2, 0), f.minus)
    to_sibling((3, 0), (1, 0))
    for f in both:
        arrive(f, "q++", "q--")
        hop(f, "xq2", (2, 0), HALF, SHARE, (2, 1), f.pair)
    for f in both:
        arrive(f, "p++", "p--")
    to_sibling((2, 0))
    arrive(images, "xq")
    to_sibling((0, 1))
    arrive(texts, "xq")

    def weigh(first_text, first_image, count):
        @pl.loop(first_image, first_image + count)
        def _(ii):
            columns = pl.ds(pl.multiple_of(ii * 2 * SHARE, 2 * SHARE), 2 * SHARE)
            scores = lax.dot_general(
                captions[pl.ds(first_text * SHARE, 4 * SHARE), :], pictures[columns, :],
                (((1,), (1,)), ((), ())), preferred_element_type=jnp.float32,
            )
            label = jnp.concatenate([labels[2 * ii, :1, :], labels[2 * ii + 1, :1, :]], axis=1)
            ids = lax.broadcasted_iota(jnp.int32, (SHARE, 2 * SHARE), 0)
            for j in range(4):
                own = ids == label - starts[first_text + j]
                part = scores[j * SHARE : (j + 1) * SHARE] * half_sharp + half_shift
                twice = jnp.tanh(part) + jnp.where(own, -1.0, 1.0)
                weights[pl.ds((first_text + j) * SHARE, SHARE), columns] = twice.astype(jnp.bfloat16)

    arrive(images, ("s", (0, 0)), ("s", (3, 0)), ("s", (1, 0)), ("s", (2, 0)))
    weigh(0, 0, 4)
    for f in both:
        arrive(f, "P+", "P-")
        hop(f, "P++", (3, 1), 0, mid_p, (2, 1), f.plus)
        hop(f, "P--", (1, 1), mid_p, HALF, (2, 1), f.minus)
    arrive(images, "xq1", "xq3")
    to_sibling((3, 1), (1, 1))
    arrive(images, ("s", (0, 1)), ("s", (3, 1)), ("s", (1, 1)))
    weigh(0, 4, 3)
    arrive(images, "P++", "P--", "xq2")
    to_sibling((2, 1))
    arrive(texts, "xq1", "xq3", "P++", "P--", "xq2")
    weigh(4, 0, 7)
    arrive(images, ("s", (2, 1)))
    weigh(0, 7, 1)
    weigh(4, 7, 1)

    def multiply_pictures(key):
        rows = pl.ds(SLOT[key] * 2 * SHARE, 2 * SHARE)
        picture_sums[rows, :] = lax.dot_general(
            weights[:, rows], captions[...], (((0,), (0,)), ((), ())), preferred_element_type=jnp.float32
        )
        images.sent["t", key] = send(
            picture_sums.at[pl.ds(SLOT[key] * 2 * SHARE + SHARE, SHARE)], sibling_sums.at[SLOT[key]], sibling
        )

    def multiply_captions(key):
        rows = pl.ds(SLOT[key] * SHARE, SHARE)
        caption_sums[rows, :] = jnp.dot(weights[rows, :], pictures[...], preferred_element_type=jnp.float32)

    lanes = lax.broadcasted_iota(jnp.int32, (8, 128), 1)

    def unpacked(index, at):
        scale = in_scale[index]
        column = jnp.concatenate([scale[:, k : k + 1] for k in range(at // 8, (at + UNIT) // 8)], axis=0)
        return in_data[index, pl.ds(at, UNIT), :].astype(jnp.int32).astype(jnp.float32) * column

    def total(f, key, lo, arrived):
        x = f.sums[pl.ds(SLOT[key] * f.step + lo, UNIT), :]
        if f.other is not None:
            x = x + f.other[SLOT[key], pl.ds(lo, UNIT), :]
        for index, at in arrived:
            x = x + unpacked(index, at)
        return x

    def pass_on(f, name, key, lo, hi, arrived, device):
        index = f.message
        f.message += 1
        scale = jnp.zeros((8, 128), jnp.float32)
        for row in range(lo, hi, UNIT):
            x = total(f, key, row, arrived(row))
            peak = jnp.maximum(jnp.max(jnp.abs(x), axis=1, keepdims=True), 1e-30)
            whole = x * (TOP / peak)
            whole = (whole + 12582912.0) - 12582912.0
            out_data[index, pl.ds(row - lo, UNIT), :] = whole.astype(jnp.int32).astype(jnp.int16)
            for k in range(UNIT // 8):
                scale = jnp.where(lanes == (row - lo) // 8 + k, peak[8 * k : 8 * k + 8] * (1.0 / TOP), scale)
        out_scale[index] = scale
        span = pl.ds(0, hi - lo)
        data = send(out_data.at[index, span], in_data.at[index, span], device)
        f.sent[name] = (index, lo, hi, data, send(out_scale.at[index], in_scale.at[index], device))

    def landed(f, *names):
        for name in names:
            for copy in f.sent[name][3:]:
                copy.wait_recv()

    def came(f, *names):
        whole = [f.sent[name][:3] for name in names]
        return lambda row: [(i, row - lo) for i, lo, hi in whole if lo <= row < hi]

    def ring(f, d, dx, tag, lo, also=()):
        mid, hi = lo + HALF // 2, lo + HALF
        if d == 2:
            pass_on(f, tag + "a", (2, dx), lo, mid, came(f, *also), f.plus)
            pass_on(f, tag + "b", (2, dx), mid, hi, came(f, *also), f.minus)
        if d == 1:
            landed(f, tag + "a")
            pass_on(f, tag + "c", (1, dx), lo, hi, came(f, tag + "a", *also), f.plus)
        if d == 3:
            landed(f, tag + "b")
            pass_on(f, tag + "d", (3, dx), lo, hi, came(f, tag + "b", *also), f.minus)

    def reduce(f, key):
        d, dx = key
        if dx == 1:
            pass_on(f, f"x{d}", key, HALF, SHARE, came(f), f.pair)
            ring(f, d, 1, "P", 0)
            if d == 0:
                landed(f, "Pc", "Pd")
                pass_on(f, "xp'", key, 0, HALF, came(f, "Pc", "Pd"), f.pair)
            return
        ring(f, d, 0, "p", 0)
        landed(f, f"x{d}")
        ring(f, d, 0, "q", HALF, (f"x{d}",))
        if d == 0:
            landed(f, "pc", "pd", "qc", "qd", "xp'")
            for lo, names in ((0, ("pc", "pd", "xp'")), (HALF, ("x0", "qc", "qd"))):
                for row in range(lo, lo + HALF, UNIT):
                    f.out[pl.ds(row, UNIT), :] = total(f, key, row, came(f, *names)(row))

    for key in [(2, 1), (1, 1), (3, 1), (0, 1), (2, 0), (1, 0), (3, 0), (0, 0)]:
        multiply_pictures(key)
        multiply_captions(key)
        reduce(texts, key)
        arrive(images, ("t", key))
        reduce(images, key)
    for copy in copies:
        copy.wait_send()


COPIES = 34 + 8 + 8 + 8 + 4 * MESSAGES


def per_device(picture_vectors, caption_vectors, matching_caption, sharpness_parameter, additive_intercept):
    width = picture_vectors.shape[1]
    f32, bf16 = jnp.float32, jnp.bfloat16
    out = jax.ShapeDtypeStruct((SHARE, width), f32)
    vmem, smem = pl.BlockSpec(memory_space=pltpu.VMEM), pl.BlockSpec(memory_space=pltpu.SMEM)
    anywhere = pl.BlockSpec(memory_space=pl.ANY)
    picture_sums, caption_sums = pl.pallas_call(
        kernel,
        out_shape=(out, out),
        in_specs=[smem, smem, anywhere, anywhere, vmem],
        out_specs=(vmem, vmem),
        scratch_shapes=[
            pltpu.VMEM((16 * SHARE, width), bf16),
            pltpu.VMEM((8 * SHARE, width), bf16),
            pltpu.VMEM((16, 8, SHARE), jnp.int32),
            pltpu.VMEM((8 * SHARE, 16 * SHARE), bf16),
            pltpu.VMEM((16 * SHARE, width), f32),
            pltpu.VMEM((8 * SHARE, width), f32),
            pltpu.VMEM((8, SHARE, width), f32),
            pltpu.VMEM((2 * MESSAGES, HALF, width), jnp.int16),
            pltpu.VMEM((2 * MESSAGES, HALF, width), jnp.int16),
            pltpu.VMEM((2 * MESSAGES, 8, 128), f32),
            pltpu.VMEM((2 * MESSAGES, 8, 128), f32),
            pltpu.SemaphoreType.DMA((2,)),
            pltpu.SemaphoreType.DMA((COPIES,)),
            pltpu.SemaphoreType.DMA((COPIES,)),
        ],
        compiler_params=pltpu.CompilerParams(
            collective_id=0, has_side_effects=True, vmem_limit_bytes=60 * 2**20
        ),
        cost_estimate=pl.CostEstimate(
            flops=6 * 2048 * 1024 * width, bytes_accessed=6 * SHARE * width * 2, transcendentals=2048 * 1024
        ),
        name="pair_loss_backward",
    )(sharpness_parameter, additive_intercept, picture_vectors, caption_vectors, matching_caption[None, :])
    scale = 0.5 * sharpness_parameter[0]
    return scale * picture_sums, scale * caption_sums


def solution(mesh):
    placed = (P(("blk", "grp"), None), P(("blk", "grp"), None), P(("blk", "grp")), P(), P())
    return jax.shard_map(
        per_device,
        mesh=mesh,
        in_specs=placed,
        out_specs=(P(("blk", "grp"), None), P(("blk", "grp"), None)),
        check_vma=False,
    )
```

```python
import functools

import jax
import jax.numpy as jnp
from jax import lax
from jax.experimental import pallas as pl
from jax.experimental.pallas import tpu as pltpu
from jax.sharding import PartitionSpec as P

MESH = pl.DeviceIdType.MESH
ORDER = [(0, 0), (3, 0), (1, 0), (0, 1), (2, 0), (3, 1), (1, 1), (2, 1)]
SLOT = {key: i for i, key in enumerate(ORDER)}
EARLY = 5
SHARE = 128
HALF = 64
UNIT = 32
TOP = 32767.0

ROUTE = {}
RESULT = {}
for part, at in (("A", 0), ("B", UNIT)):
    for step in range(4):
        ROUTE[f"x{step}{part}"] = ((step, 1), HALF + at, "pair", ())
    ROUTE["y" + part] = ((0, 1), at, "pair", ("Pc" + part, "Pd" + part))
    RESULT["oP" + part] = (at, ("pc" + part, "pd" + part, "y" + part))
    RESULT["oQ" + part] = (HALF + at, ("qc" + part, "qd" + part, "x0" + part))
    for tag, dx, low in (("P", 1, 0), ("p", 0, 0), ("q", 0, HALF)):
        came = lambda step: (f"x{step}{part}",) if tag == "q" else ()
        far, way = ("a", "plus") if part == "A" else ("b", "minus")
        ROUTE[tag + far] = ((2, dx), low + at, way, came(2))
        ROUTE[tag + "c" + part] = ((1, dx), low + at, "plus", came(1) + ((tag + "a",) if part == "A" else ()))
        ROUTE[tag + "d" + part] = ((3, dx), low + at, "minus", came(3) + ((tag + "b",) if part == "B" else ()))
NUMBER = {name: i for i, name in enumerate(ROUTE)}

PLAN = [
    "V3", "V7", "V4", "W7", "V1", "V2", "V5", "mp34", "V6", "mp76", "sh7", "sh4", "V0", "mc567", "tx2A",
    "ix2B", "tPcB", "iPa", "tPb", "tPdA", "tx1A", "tPa", "ix2A", "ipb", "tx2B", "sh6", "tx3A", "iPb", "mp5",
    "sh5", "tx3B", "ipa", "ix1B", "mc34", "iPcA", "tPdB", "tqa", "iPdA", "iqb", "tx0B", "ix3B", "tpb", "tPcA",
    "iqa", "ix3A", "tpa", "sh3", "mp12", "tqb", "sh1", "sh2", "tx1B", "iPdB", "ix1A", "ix0A", "tyB", "ix0B",
    "iPcB", "mc12", "tpdA", "tqcA", "tpdB", "iqdB", "iqcB", "tyA", "ipdB", "tpcB", "tqdA", "iqdA", "tqdB",
    "ipcB", "tpcA", "iyB", "iqcA", "ipcA", "ipdA", "mc0", "mp0", "sh0", "tqcB", "tx0A", "iyA", "toPB", "ioQB",
    "toPA", "ioPB", "ioQA", "toQB", "toQA", "ioPA",
]


def peers():
    b, g = lax.axis_index("blk"), lax.axis_index("grp")
    xl, y = b // 4, lax.rem(b, 4)
    z, low = g // 4, lax.rem(g, 4)
    xh, core = low // 2, lax.rem(low, 2)

    def at(xl, y, z, xh, core):
        return (xl * 4 + y, z * 4 + xh * 2 + core)

    up = lambda v: lax.rem(v + 1, 4)
    down = lambda v: lax.rem(v + 3, 4)
    pictures = (at(xl, y, up(z), xh, core), at(xl, y, down(z), xh, core), at(1 - xl, y, z, xh, core))
    captions = (at(xl, up(y), z, xh, core), at(xl, down(y), z, xh, core), at(1 - xl, y, z, 1 - xh, core))
    sibling = at(xl, y, z, xh, 1 - core)
    starts = []
    for dy, dx in ORDER:
        txl = 1 - xl if dx else xl
        txh = 1 - xh if dx else xh
        blk, grp = at(txl, lax.rem(y + dy, 4), z, txh, core)
        starts.append((blk * 16 + grp) * SHARE)
    return pictures, captions, sibling, starts


class Family:
    def __init__(self, shares, step, sums, other, devices, out, first):
        self.shares, self.step, self.sums, self.other = shares, step, sums, other
        self.plus, self.minus, self.pair = devices
        self.out, self.first = out, first
        self.sent = {}

    def rows(self, key, lo, hi):
        return self.shares.at[pl.ds(SLOT[key] * self.step + lo, hi - lo)]


def kernel(
    sharp_ref, shift_ref, picture_ref, caption_ref, label_ref, picture_out, caption_out,
    pictures, captions, labels, weights, picture_sums, caption_sums, sibling_sums,
    out_data, in_data, out_scale, in_scale, local_sem, send_sem, recv_sem,
):
    picture_peers, caption_peers, sibling, starts = peers()
    loads = [
        pltpu.make_async_copy(picture_ref, pictures.at[pl.ds(0, SHARE)], local_sem.at[0]),
        pltpu.make_async_copy(caption_ref, captions.at[pl.ds(0, SHARE)], local_sem.at[1]),
    ]
    for load in loads:
        load.start()
    barrier = pltpu.get_barrier_semaphore()
    everyone = [*picture_peers, *caption_peers, sibling]
    for device in everyone:
        pl.semaphore_signal(barrier, inc=1, device_id=device, device_id_type=MESH)
    labels[0] = jnp.broadcast_to(label_ref[...], (8, SHARE))
    half_sharp = sharp_ref[0] * 0.5
    half_shift = shift_ref[0] * 0.5
    for load in loads:
        load.wait()
    pl.semaphore_wait(barrier, len(everyone))

    width = picture_ref.shape[1]
    copies = []

    def send(src, dst, device):
        i = len(copies)
        copy = pltpu.make_async_remote_copy(
            src_ref=src, dst_ref=dst, send_sem=send_sem.at[i], recv_sem=recv_sem.at[i],
            device_id=device, device_id_type=MESH,
        )
        copy.start()
        copies.append(copy)
        return copy

    images = Family(pictures, 2 * SHARE, picture_sums, sibling_sums, picture_peers, picture_out, 0)
    texts = Family(captions, SHARE, caption_sums, None, caption_peers, caption_out, len(ROUTE))
    both = (images, texts)
    mid_p, mid_q = HALF // 2, HALF + HALF // 2

    def hop(f, name, key, lo, hi, to, device):
        f.sent[name] = send(f.rows(key, lo, hi), f.rows(to, lo, hi), device)

    def label_hop(name, key, to, device):
        images.sent[name] = send(labels.at[2 * SLOT[key]], labels.at[2 * SLOT[to]], device)

    def to_sibling(*keys):
        for key in keys:
            start = SLOT[key] * 2 * SHARE
            images.sent["s", key] = send(
                pictures.at[pl.ds(start, SHARE)], pictures.at[pl.ds(start + SHARE, SHARE)], sibling
            )
            images.sent["l", key] = send(labels.at[2 * SLOT[key]], labels.at[2 * SLOT[key] + 1], sibling)

    def arrive(f, *names):
        for name in names:
            f.sent[name].wait_recv()

    def from_sibling(*keys):
        for key in keys:
            arrive(images, ("s", key), ("l", key))

    def around(f, tag, key, to_plus, to_minus, lo):
        mid, hi = lo + HALF // 2, lo + HALF
        hop(f, tag + "+a", key, lo, mid, to_plus, f.plus)
        hop(f, tag + "-b", key, mid, hi, to_minus, f.minus)
        hop(f, tag + "+b", key, mid, hi, to_plus, f.plus)
        hop(f, tag + "-a", key, lo, mid, to_minus, f.minus)

    def onward(f, tag, dx, lo):
        arrive(f, tag + "+a", tag + "-b")
        hop(f, tag + "++", (3, dx), lo, lo + HALF // 2, (2, dx), f.plus)
        hop(f, tag + "--", (1, dx), lo + HALF // 2, lo + HALF, (2, dx), f.minus)

    to_sibling((0, 0))
    for f in both:
        around(f, "q", (0, 0), (3, 0), (1, 0), HALF)
        hop(f, "xp", (0, 0), 0, HALF, (0, 1), f.pair)
    label_hop("xl", (0, 0), (0, 1), images.pair)
    label_hop("l+", (0, 0), (3, 0), images.plus)
    label_hop("l-", (0, 0), (1, 0), images.minus)
    for f in both:
        around(f, "p", (0, 0), (3, 0), (1, 0), 0)
        hop(f, "xq", (0, 0), HALF, SHARE, (0, 1), f.pair)
    for f in both:
        onward(f, "q", 0, HALF)
    for f in both:
        arrive(f, "q+b", "q-a")
        hop(f, "xq1", (1, 0), HALF, SHARE, (1, 1), f.pair)
        hop(f, "xq3", (3, 0), HALF, SHARE, (3, 1), f.pair)
    arrive(images, "l+", "l-", "xl")
    label_hop("l++", (3, 0), (2, 0), images.plus)
    label_hop("L+", (0, 1), (3, 1), images.plus)
    label_hop("L-", (0, 1), (1, 1), images.minus)
    for f in both:
        onward(f, "p", 0, 0)
    for f in both:
        arrive(f, "xp")
        around(f, "P", (0, 1), (3, 1), (1, 1), 0)
    arrive(images, "p+b", "p-a")
    to_sibling((3, 0), (1, 0))
    arrive(images, "xq")
    to_sibling((0, 1))
    arrive(texts, "p+b", "p-a", "xq")
    arrive(images, "L+", "L-")
    label_hop("L++", (3, 1), (2, 1), images.plus)
    for f in both:
        arrive(f, "q++", "q--")
        hop(f, "xq2", (2, 0), HALF, SHARE, (2, 1), f.pair)

    def weigh(first_text, texts, first_image, images):
        @pl.loop(first_image, first_image + images)
        def _(ii):
            columns = pl.ds(pl.multiple_of(ii * 2 * SHARE, 2 * SHARE), 2 * SHARE)
            scores = lax.dot_general(
                captions[pl.ds(first_text * SHARE, texts * SHARE), :], pictures[columns, :],
                (((1,), (1,)), ((), ())), preferred_element_type=jnp.float32,
            )
            label = jnp.concatenate([labels[2 * ii, :1, :], labels[2 * ii + 1, :1, :]], axis=1)
            ids = lax.broadcasted_iota(jnp.int32, (SHARE, 2 * SHARE), 0)
            for j in range(texts):
                own = ids == label - starts[first_text + j]
                part = scores[j * SHARE : (j + 1) * SHARE] * half_sharp + half_shift
                twice = jnp.tanh(part) + jnp.where(own, -1.0, 1.0)
                weights[pl.ds((first_text + j) * SHARE, SHARE), columns] = twice.astype(jnp.bfloat16)

    def add(sums, rows, value, more):
        sums[rows, :] = sums[rows, :] + value if more else value

    def multiply_pictures(first, count, lo, hi, more=False):
        rows, inner = pl.ds(first * 2 * SHARE, count * 2 * SHARE), pl.ds(lo * SHARE, (hi - lo) * SHARE)
        value = lax.dot_general(
            weights[inner, rows], captions[inner, :], (((0,), (0,)), ((), ())), preferred_element_type=jnp.float32
        )
        add(picture_sums, rows, value, more)

    def multiply_captions(first, count, lo, hi, more=False):
        rows, inner = pl.ds(first * SHARE, count * SHARE), pl.ds(lo * 2 * SHARE, (hi - lo) * 2 * SHARE)
        value = jnp.dot(weights[rows, inner], pictures[inner, :], preferred_element_type=jnp.float32)
        add(caption_sums, rows, value, more)

    from_sibling((0, 0), (3, 0), (1, 0), (0, 1))
    for f in both:
        arrive(f, "p++", "p--")
    arrive(images, "l++")
    to_sibling((2, 0))
    weigh(0, EARLY, 0, 4)
    for f in both:
        onward(f, "P", 1, 0)
    from_sibling((2, 0))
    weigh(0, EARLY, 4, 1)
    multiply_captions(0, EARLY, 0, EARLY)
    for f in both:
        arrive(f, "P+b", "P-a", "xq1", "xq3")
    to_sibling((3, 1), (1, 1))
    multiply_pictures(0, EARLY, 0, EARLY)
    from_sibling((3, 1), (1, 1))
    arrive(images, "P++", "P--", "L++", "xq2")
    to_sibling((2, 1))
    weigh(0, EARLY, 5, 2)
    arrive(texts, "P++", "P--", "xq2")
    from_sibling((2, 1))

    def wide(tile):
        return jnp.concatenate([jnp.concatenate([tile] * (width // 128), axis=1)] * (UNIT // 8), axis=0)

    landed = set()

    def land(f, names):
        for name in names:
            if (f, name) not in landed:
                landed.add((f, name))
                for copy in f.sent[name]:
                    copy.wait_recv()

    def total(f, key, lo, names):
        x = f.sums[pl.ds(SLOT[key] * f.step + lo, UNIT), :]
        if f.other is not None:
            land(f, [f"sh{SLOT[key]}"])
            x = x + f.other[SLOT[key], pl.ds(lo, UNIT), :]
        land(f, names)
        for name in names:
            index = f.first + NUMBER[name]
            x = x + in_data[index].astype(jnp.int32).astype(jnp.float32) * wide(in_scale[index])
        return x

    def pass_on(f, name):
        key, lo, way, names = ROUTE[name]
        index = f.first + NUMBER[name]
        x = total(f, key, lo, names)
        size = jnp.abs(x)
        peak = jnp.full((8, 128), 1e-30, jnp.float32)
        for r in range(0, UNIT, 8):
            for c in range(0, width, 128):
                peak = jnp.maximum(peak, size[r : r + 8, c : c + 128])
        out_data[index] = jnp.round(x * wide(TOP / peak)).astype(jnp.int32).astype(jnp.int16)
        out_scale[index] = peak * (1.0 / TOP)
        device = getattr(f, way)
        f.sent[name] = (
            send(out_data.at[index], in_data.at[index], device),
            send(out_scale.at[index], in_scale.at[index], device),
        )

    def work(name):
        slots = [int(digit) for digit in name[2:] if digit.isdigit()]
        if name == "W7":
            weigh(0, EARLY, 7, 1)
        elif name[0] == "V":
            weigh(EARLY, 8 - EARLY, int(name[1]), 1)
        elif name[:2] in ("mp", "mc"):
            multiply = multiply_pictures if name[1] == "p" else multiply_captions
            begun = min(slots) < EARLY
            multiply(min(slots), len(slots), EARLY if begun else 0, 8, begun)
        elif name[:2] == "sh":
            i = slots[0]
            rows = pl.ds(i * 2 * SHARE + SHARE, SHARE)
            images.sent[name] = (send(picture_sums.at[rows], sibling_sums.at[i], sibling),)
        else:
            f = images if name[0] == "i" else texts
            if name[1:] in ROUTE:
                pass_on(f, name[1:])
            else:
                lo, names = RESULT[name[1:]]
                f.out[pl.ds(lo, UNIT), :] = total(f, (0, 0), lo, names)

    for name in PLAN:
        work(name)
    for copy in copies:
        copy.wait_send()


COPIES = 46 + 16 + 7 + 8 + 4 * len(ROUTE)


def per_device(picture_vectors, caption_vectors, matching_caption, sharpness_parameter, additive_intercept):
    width = picture_vectors.shape[1]
    f32, bf16 = jnp.float32, jnp.bfloat16
    out = jax.ShapeDtypeStruct((SHARE, width), f32)
    vmem, smem = pl.BlockSpec(memory_space=pltpu.VMEM), pl.BlockSpec(memory_space=pltpu.SMEM)
    anywhere = pl.BlockSpec(memory_space=pl.ANY)
    picture_sums, caption_sums = pl.pallas_call(
        kernel,
        out_shape=(out, out),
        in_specs=[smem, smem, anywhere, anywhere, vmem],
        out_specs=(vmem, vmem),
        scratch_shapes=[
            pltpu.VMEM((16 * SHARE, width), bf16),
            pltpu.VMEM((8 * SHARE, width), bf16),
            pltpu.VMEM((16, 8, SHARE), jnp.int32),
            pltpu.VMEM((8 * SHARE, 16 * SHARE), bf16),
            pltpu.VMEM((16 * SHARE, width), f32),
            pltpu.VMEM((8 * SHARE, width), f32),
            pltpu.VMEM((8, SHARE, width), f32),
            pltpu.VMEM((2 * len(ROUTE), UNIT, width), jnp.int16),
            pltpu.VMEM((2 * len(ROUTE), UNIT, width), jnp.int16),
            pltpu.VMEM((2 * len(ROUTE), 8, 128), f32),
            pltpu.VMEM((2 * len(ROUTE), 8, 128), f32),
            pltpu.SemaphoreType.DMA((2,)),
            pltpu.SemaphoreType.DMA((COPIES,)),
            pltpu.SemaphoreType.DMA((COPIES,)),
        ],
        compiler_params=pltpu.CompilerParams(
            collective_id=0, has_side_effects=True, vmem_limit_bytes=60 * 2**20
        ),
        cost_estimate=pl.CostEstimate(
            flops=6 * 2048 * 1024 * width, bytes_accessed=6 * SHARE * width * 2, transcendentals=2048 * 1024
        ),
        name="pair_loss_backward",
    )(sharpness_parameter, additive_intercept, picture_vectors, caption_vectors, matching_caption[None, :])
    scale = 0.5 * sharpness_parameter[0]
    return scale * picture_sums, scale * caption_sums


def solution(mesh):
    placed = (P(("blk", "grp"), None), P(("blk", "grp"), None), P(("blk", "grp")), P(), P())
    return jax.shard_map(
        per_device,
        mesh=mesh,
        in_specs=placed,
        out_specs=(P(("blk", "grp"), None), P(("blk", "grp"), None)),
        check_vma=False,
    )
```

```python
import functools

import jax
import jax.numpy as jnp
from jax import lax
from jax.experimental import pallas as pl
from jax.experimental.pallas import tpu as pltpu
from jax.sharding import PartitionSpec as P

MESH = pl.DeviceIdType.MESH
ORDER = [(0, 0), (3, 0), (1, 0), (0, 1), (2, 0), (3, 1), (1, 1), (2, 1)]
SLOT = {key: i for i, key in enumerate(ORDER)}
EARLY = 5
SHARE = 128
HALF = 64
UNIT = 32
TILES = 9
TOP = 32760.0

ROUTE = {}
RESULT = {}
for part, at in (("A", 0), ("B", UNIT)):
    for step in range(4):
        ROUTE[f"x{step}{part}"] = ((step, 1), HALF + at, "pair", ())
    ROUTE["y" + part] = ((0, 1), at, "pair", ("Pc" + part, "Pd" + part))
    RESULT["oP" + part] = (at, ("pc" + part, "pd" + part, "y" + part))
    RESULT["oQ" + part] = (HALF + at, ("qc" + part, "qd" + part, "x0" + part))
    for tag, dx, low in (("P", 1, 0), ("p", 0, 0), ("q", 0, HALF)):
        came = lambda step: (f"x{step}{part}",) if tag == "q" else ()
        far, way = ("a", "plus") if part == "A" else ("b", "minus")
        ROUTE[tag + far] = ((2, dx), low + at, way, came(2))
        ROUTE[tag + "c" + part] = ((1, dx), low + at, "plus", came(1) + ((tag + "a",) if part == "A" else ()))
        ROUTE[tag + "d" + part] = ((3, dx), low + at, "minus", came(3) + ((tag + "b",) if part == "B" else ()))
NUMBER = {name: i for i, name in enumerate(ROUTE)}

PLAN = [
    "V4", "V2", "V7", "V6", "W7", "mp76", "sh6p", "sh7q", "V5", "sh7p", "mc12", "tpdA", "iPcB", "mc34",
    "tx0B", "ix2A", "V1", "iPb", "iPa", "tx0A", "mp5", "sh5p", "sh5q", "ix2B", "sh6q", "tpb", "tpcB", "V3",
    "V0", "mc7", "tx2A", "tPa", "tPb", "ix3A", "tx2B", "iPdA", "ix1A", "ix1B", "mp12", "sh2q", "sh1q", "sh1p",
    "mp4", "sh4q", "sh4p", "iPcA", "tpdB", "tpa", "iPdB", "ix3B", "mc56", "tx3B", "tPcB", "tPdA", "ipdA",
    "tPcA", "tx3A", "iqa", "iqdA", "iqb", "tqa", "tx1B", "mc0", "ipb", "ipa", "sh2p", "mp3", "sh3q", "tPdB",
    "mp0", "tqb", "tpcA", "ipcB", "sh0q", "sh0p", "sh3p", "tx1A", "ix0A", "ix0B", "iqcB", "iqcA", "iyB",
    "iyA", "tyB", "tqdA", "tyA", "ipcA", "tqdB", "tqcB", "iqdB", "tqcA", "ipdB", "toPB", "toQB", "ioQA",
    "ioQB", "toPA", "toQA", "ioPB", "ioPA",
]


def peers():
    b, g = lax.axis_index("blk"), lax.axis_index("grp")
    xl, y = b // 4, lax.rem(b, 4)
    z, low = g // 4, lax.rem(g, 4)
    xh, core = low // 2, lax.rem(low, 2)

    def at(xl, y, z, xh, core):
        return (xl * 4 + y, z * 4 + xh * 2 + core)

    up = lambda v: lax.rem(v + 1, 4)
    down = lambda v: lax.rem(v + 3, 4)
    pictures = (at(xl, y, up(z), xh, core), at(xl, y, down(z), xh, core), at(1 - xl, y, z, xh, core))
    captions = (at(xl, up(y), z, xh, core), at(xl, down(y), z, xh, core), at(1 - xl, y, z, 1 - xh, core))
    sibling = at(xl, y, z, xh, 1 - core)
    starts = []
    for dy, dx in ORDER:
        txl = 1 - xl if dx else xl
        txh = 1 - xh if dx else xh
        blk, grp = at(txl, lax.rem(y + dy, 4), z, txh, core)
        starts.append((blk * 16 + grp) * SHARE)
    return pictures, captions, sibling, starts


class Family:
    def __init__(self, shares, step, sums, other, devices, out, first):
        self.shares, self.step, self.sums, self.other = shares, step, sums, other
        self.plus, self.minus, self.pair = devices
        self.out, self.first = out, first
        self.sent = {}

    def rows(self, key, lo, hi):
        return self.shares.at[pl.ds(SLOT[key] * self.step + lo, hi - lo)]


def kernel(
    sharp_ref, shift_ref, picture_ref, caption_ref, label_ref, picture_out, caption_out,
    pictures, captions, own_labels, labels, weights, picture_sums, caption_sums, sibling_sums,
    out_data, in_data, local_sem, send_sem, recv_sem,
):
    picture_peers, caption_peers, sibling, starts = peers()
    loads = [
        pltpu.make_async_copy(picture_ref, pictures.at[pl.ds(0, SHARE)], local_sem.at[0]),
        pltpu.make_async_copy(caption_ref, captions.at[pl.ds(0, SHARE)], local_sem.at[1]),
        pltpu.make_async_copy(label_ref, own_labels, local_sem.at[2]),
    ]
    for load in loads:
        load.start()
    barrier = pltpu.get_barrier_semaphore()
    everyone = [*picture_peers, *caption_peers, sibling]
    for device in everyone:
        pl.semaphore_signal(barrier, inc=1, device_id=device, device_id_type=MESH)
    half_sharp = sharp_ref[0] * 0.5
    half_shift = shift_ref[0] * 0.5
    for load in loads:
        load.wait()
    labels[0] = jnp.broadcast_to(own_labels[...], (8, SHARE))
    pl.semaphore_wait(barrier, len(everyone))

    width = picture_ref.shape[1]
    copies = []

    def send(src, dst, device):
        i = len(copies)
        copy = pltpu.make_async_remote_copy(
            src_ref=src, dst_ref=dst, send_sem=send_sem.at[i], recv_sem=recv_sem.at[i],
            device_id=device, device_id_type=MESH,
        )
        copy.start()
        copies.append(copy)
        return copy

    images = Family(pictures, 2 * SHARE, picture_sums, sibling_sums, picture_peers, picture_out, 0)
    texts = Family(captions, SHARE, caption_sums, None, caption_peers, caption_out, len(ROUTE))
    both = (images, texts)
    mid_p, mid_q = HALF // 2, HALF + HALF // 2

    def hop(f, name, key, lo, hi, to, device):
        f.sent[name] = send(f.rows(key, lo, hi), f.rows(to, lo, hi), device)

    def label_hop(name, key, to, device):
        images.sent[name] = send(labels.at[2 * SLOT[key]], labels.at[2 * SLOT[to]], device)

    def to_sibling(*keys):
        for key in keys:
            start = SLOT[key] * 2 * SHARE
            images.sent["s", key] = send(
                pictures.at[pl.ds(start, SHARE)], pictures.at[pl.ds(start + SHARE, SHARE)], sibling
            )
            images.sent["l", key] = send(labels.at[2 * SLOT[key]], labels.at[2 * SLOT[key] + 1], sibling)

    def arrive(f, *names):
        for name in names:
            f.sent[name].wait_recv()

    def from_sibling(*keys):
        for key in keys:
            arrive(images, ("s", key), ("l", key))

    def around(f, tag, key, to_plus, to_minus, lo):
        mid, hi = lo + HALF // 2, lo + HALF
        hop(f, tag + "+a", key, lo, mid, to_plus, f.plus)
        hop(f, tag + "-b", key, mid, hi, to_minus, f.minus)
        hop(f, tag + "+b", key, mid, hi, to_plus, f.plus)
        hop(f, tag + "-a", key, lo, mid, to_minus, f.minus)

    def onward(f, tag, dx, lo):
        arrive(f, tag + "+a", tag + "-b")
        hop(f, tag + "++", (3, dx), lo, lo + HALF // 2, (2, dx), f.plus)
        hop(f, tag + "--", (1, dx), lo + HALF // 2, lo + HALF, (2, dx), f.minus)

    to_sibling((0, 0))
    for f in both:
        around(f, "q", (0, 0), (3, 0), (1, 0), HALF)
        hop(f, "xp", (0, 0), 0, HALF, (0, 1), f.pair)
    label_hop("xl", (0, 0), (0, 1), images.pair)
    label_hop("l+", (0, 0), (3, 0), images.plus)
    label_hop("l-", (0, 0), (1, 0), images.minus)
    for f in both:
        around(f, "p", (0, 0), (3, 0), (1, 0), 0)
        hop(f, "xq", (0, 0), HALF, SHARE, (0, 1), f.pair)
    for f in both:
        onward(f, "q", 0, HALF)
    for f in both:
        arrive(f, "q+b", "q-a")
        hop(f, "xq1", (1, 0), HALF, SHARE, (1, 1), f.pair)
        hop(f, "xq3", (3, 0), HALF, SHARE, (3, 1), f.pair)
    arrive(images, "l+", "l-", "xl")
    label_hop("l++", (3, 0), (2, 0), images.plus)
    label_hop("L+", (0, 1), (3, 1), images.plus)
    label_hop("L-", (0, 1), (1, 1), images.minus)
    for f in both:
        onward(f, "p", 0, 0)
    for f in both:
        arrive(f, "xp")
        around(f, "P", (0, 1), (3, 1), (1, 1), 0)
    arrive(images, "p+b", "p-a")
    to_sibling((3, 0), (1, 0))
    arrive(images, "xq")
    to_sibling((0, 1))
    arrive(texts, "p+b", "p-a", "xq")
    arrive(images, "L+", "L-")
    label_hop("L++", (3, 1), (2, 1), images.plus)
    for f in both:
        arrive(f, "q++", "q--")
        hop(f, "xq2", (2, 0), HALF, SHARE, (2, 1), f.pair)

    def weigh(first_text, texts, first_image, images):
        @pl.loop(first_image, first_image + images)
        def _(ii):
            columns = pl.ds(pl.multiple_of(ii * 2 * SHARE, 2 * SHARE), 2 * SHARE)
            scores = lax.dot_general(
                captions[pl.ds(first_text * SHARE, texts * SHARE), :], pictures[columns, :],
                (((1,), (1,)), ((), ())), preferred_element_type=jnp.float32,
            )
            label = jnp.concatenate([labels[2 * ii, :1, :], labels[2 * ii + 1, :1, :]], axis=1)
            ids = lax.broadcasted_iota(jnp.int32, (SHARE, 2 * SHARE), 0)
            for j in range(texts):
                own = ids == label - starts[first_text + j]
                part = scores[j * SHARE : (j + 1) * SHARE] * half_sharp + half_shift
                twice = jnp.tanh(part) + jnp.where(own, -1.0, 1.0)
                weights[pl.ds((first_text + j) * SHARE, SHARE), columns] = twice.astype(jnp.bfloat16)

    def add(sums, rows, value, more):
        sums[rows, :] = sums[rows, :] + value if more else value

    def multiply_pictures(first, count, lo, hi, more=False):
        rows, inner = pl.ds(first * 2 * SHARE, count * 2 * SHARE), pl.ds(lo * SHARE, (hi - lo) * SHARE)
        value = lax.dot_general(
            weights[inner, rows], captions[inner, :], (((0,), (0,)), ((), ())), preferred_element_type=jnp.float32
        )
        add(picture_sums, rows, value, more)

    def multiply_captions(first, count, lo, hi, more=False):
        rows, inner = pl.ds(first * SHARE, count * SHARE), pl.ds(lo * 2 * SHARE, (hi - lo) * 2 * SHARE)
        value = jnp.dot(weights[rows, inner], pictures[inner, :], preferred_element_type=jnp.float32)
        add(caption_sums, rows, value, more)

    from_sibling((0, 0), (3, 0), (1, 0), (0, 1))
    for f in both:
        arrive(f, "p++", "p--")
    arrive(images, "l++")
    to_sibling((2, 0))
    weigh(0, EARLY, 0, 2)
    for f in both:
        onward(f, "P", 1, 0)
    weigh(0, EARLY, 2, 2)
    from_sibling((2, 0))
    weigh(0, EARLY, 4, 1)
    multiply_captions(0, EARLY, 0, EARLY)
    for f in both:
        arrive(f, "P+b", "P-a", "xq1", "xq3")
    to_sibling((3, 1), (1, 1))
    multiply_pictures(0, EARLY, 0, EARLY)
    from_sibling((3, 1), (1, 1))
    arrive(images, "P++", "P--", "L++", "xq2")
    to_sibling((2, 1))
    weigh(0, EARLY, 5, 2)
    arrive(texts, "P++", "P--", "xq2")
    from_sibling((2, 1))

    def wide(tile):
        return jnp.concatenate([jnp.concatenate([tile] * (width // 128), axis=1)] * (UNIT // 8), axis=0)

    landed = set()

    def land(f, names):
        for name in names:
            if (f, name) not in landed:
                landed.add((f, name))
                for copy in f.sent[name]:
                    copy.wait_recv()

    def total(f, key, lo, names):
        x = f.sums[pl.ds(SLOT[key] * f.step + lo, UNIT), :]
        if f.other is not None:
            land(f, [f"sh{SLOT[key]}" + "pq"[lo // HALF]])
            x = x + f.other[SLOT[key], pl.ds(lo, UNIT), :]
        land(f, names)
        for name in names:
            index = f.first + NUMBER[name]
            rows = [jnp.concatenate([in_data[index, TILES * r + c] for c in range(TILES)], axis=1) for r in (0, 1)]
            power = in_data[index, 2 * TILES].astype(jnp.int32).astype(jnp.float32)
            scale = jnp.exp2(power[:8]) * (1.0 / TOP)
            x = x + jnp.concatenate(rows, axis=0).astype(jnp.int32).astype(jnp.float32) * wide(scale)
        return x

    def pass_on(f, name):
        key, lo, way, names = ROUTE[name]
        index = f.first + NUMBER[name]
        x = total(f, key, lo, names)
        size = jnp.abs(x)
        peak = jnp.full((8, 128), 1e-30, jnp.float32)
        for r in range(0, UNIT, 8):
            for c in range(0, width, 128):
                peak = jnp.maximum(peak, size[r : r + 8, c : c + 128])
        power = jnp.ceil(jnp.log2(peak))
        whole = jnp.round(x * wide(TOP * jnp.exp2(-power))).astype(jnp.int32).astype(jnp.int16)
        for r in (0, 1):
            for c in range(TILES):
                out_data[index, TILES * r + c] = whole[16 * r : 16 * r + 16, 128 * c : 128 * c + 128]
        out_data[index, 2 * TILES] = jnp.concatenate([power, power], axis=0).astype(jnp.int32).astype(jnp.int16)
        f.sent[name] = (send(out_data.at[index], in_data.at[index], getattr(f, way)),)

    drained = [0]

    def drain(keep):
        while drained[0] < len(copies) - keep:
            copies[drained[0]].wait_send()
            drained[0] += 1

    def work(name):
        slots = [int(digit) for digit in name[2:] if digit.isdigit()]
        if name == "W7":
            weigh(0, EARLY, 7, 1)
        elif name[0] == "V":
            weigh(EARLY, 8 - EARLY, int(name[1]), 1)
        elif name[:2] in ("mp", "mc"):
            multiply = multiply_pictures if name[1] == "p" else multiply_captions
            begun = min(slots) < EARLY
            multiply(min(slots), len(slots), EARLY if begun else 0, 8, begun)
        elif name[:2] == "sh":
            i = slots[0]
            at = HALF if name[-1] == "q" else 0
            rows = pl.ds(i * 2 * SHARE + SHARE + at, HALF)
            images.sent[name] = (send(picture_sums.at[rows], sibling_sums.at[i, pl.ds(at, HALF)], sibling),)
        else:
            f = images if name[0] == "i" else texts
            if name[1:] in ROUTE:
                pass_on(f, name[1:])
            else:
                lo, names = RESULT[name[1:]]
                drain(24)
                f.out[pl.ds(lo, UNIT), :] = total(f, (0, 0), lo, names)

    for name in PLAN:
        work(name)
    drain(0)


COPIES = 46 + 16 + 7 + 16 + 2 * len(ROUTE)


def per_device(picture_vectors, caption_vectors, matching_caption, sharpness_parameter, additive_intercept):
    width = picture_vectors.shape[1]
    f32, bf16 = jnp.float32, jnp.bfloat16
    out = jax.ShapeDtypeStruct((SHARE, width), f32)
    vmem, smem = pl.BlockSpec(memory_space=pltpu.VMEM), pl.BlockSpec(memory_space=pltpu.SMEM)
    anywhere = pl.BlockSpec(memory_space=pltpu.HBM)
    arrays = [
        pltpu.with_memory_space_constraint(array, pltpu.HBM)
        for array in (picture_vectors, caption_vectors, matching_caption[None, :])
    ]
    picture_sums, caption_sums = pl.pallas_call(
        kernel,
        out_shape=(out, out),
        in_specs=[smem, smem, anywhere, anywhere, anywhere],
        out_specs=(vmem, vmem),
        scratch_shapes=[
            pltpu.VMEM((16 * SHARE, width), bf16),
            pltpu.VMEM((8 * SHARE, width), bf16),
            pltpu.VMEM((1, SHARE), jnp.int32),
            pltpu.VMEM((16, 8, SHARE), jnp.int32),
            pltpu.VMEM((8 * SHARE, 16 * SHARE), bf16),
            pltpu.VMEM((16 * SHARE, width), f32),
            pltpu.VMEM((8 * SHARE, width), f32),
            pltpu.VMEM((8, SHARE, width), f32),
            pltpu.VMEM((2 * len(ROUTE), 2 * TILES + 1, 16, 128), jnp.int16),
            pltpu.VMEM((2 * len(ROUTE), 2 * TILES + 1, 16, 128), jnp.int16),
            pltpu.SemaphoreType.DMA((3,)),
            pltpu.SemaphoreType.DMA((COPIES,)),
            pltpu.SemaphoreType.DMA((COPIES,)),
        ],
        compiler_params=pltpu.CompilerParams(
            collective_id=0, has_side_effects=True, vmem_limit_bytes=46 * 2**20
        ),
        cost_estimate=pl.CostEstimate(
            flops=6 * 2048 * 1024 * width, bytes_accessed=6 * SHARE * width * 2, transcendentals=2048 * 1024
        ),
        name="pair_loss_backward",
    )(sharpness_parameter, additive_intercept, *arrays)
    scale = 0.5 * sharpness_parameter[0]
    return scale * picture_sums, scale * caption_sums


def solution(mesh):
    placed = (P(("blk", "grp"), None), P(("blk", "grp"), None), P(("blk", "grp")), P(), P())
    return jax.shard_map(
        per_device,
        mesh=mesh,
        in_specs=placed,
        out_specs=(P(("blk", "grp"), None), P(("blk", "grp"), None)),
        check_vma=False,
    )
```

```python
import functools

import jax
import jax.numpy as jnp
from jax import lax
from jax.experimental import pallas as pl
from jax.experimental.pallas import tpu as pltpu
from jax.sharding import PartitionSpec as P

MESH = pl.DeviceIdType.MESH
ORDER = [(0, 0), (3, 0), (1, 0), (0, 1), (2, 0), (3, 1), (1, 1), (2, 1)]
SLOT = {key: i for i, key in enumerate(ORDER)}
EARLY = 5
SHARE = 128
HALF = 64
UNIT = 32
TILES = 9
TOP = 32760.0

ROUTE = {}
RESULT = {}
for part, at in (("A", 0), ("B", UNIT)):
    for step in range(4):
        ROUTE[f"x{step}{part}"] = ((step, 1), HALF + at, "pair", ())
    ROUTE["y" + part] = ((0, 1), at, "pair", ("Pc" + part, "Pd" + part))
    RESULT["oP" + part] = (at, ("pc" + part, "pd" + part, "y" + part))
    RESULT["oQ" + part] = (HALF + at, ("qc" + part, "qd" + part, "x0" + part))
    for tag, dx, low in (("P", 1, 0), ("p", 0, 0), ("q", 0, HALF)):
        came = lambda step: (f"x{step}{part}",) if tag == "q" else ()
        far, way = ("a", "plus") if part == "A" else ("b", "minus")
        ROUTE[tag + far] = ((2, dx), low + at, way, came(2))
        ROUTE[tag + "c" + part] = ((1, dx), low + at, "plus", came(1) + ((tag + "a",) if part == "A" else ()))
        ROUTE[tag + "d" + part] = ((3, dx), low + at, "minus", came(3) + ((tag + "b",) if part == "B" else ()))
NUMBER = {name: i for i, name in enumerate(ROUTE)}

PLAN = [
    "V4", "V1", "W7", "V0", "V6", "V3", "V7", "mp76", "sh7q", "sh7p", "sh6p", "sh6q", "mc34", "tx0B", "tpa",
    "mp1", "iPb", "iPa", "ix2B", "sh1p", "ix2A", "mp4", "sh4p", "iPcB", "ix1B", "sh4q", "tx0A", "tpb", "V2",
    "ipdA", "V5", "ipa", "mc7", "tPa", "tx2A", "tPb", "ipb", "mp5", "sh5q", "tx2B", "ix1A", "sh5p", "mc12",
    "tpcB", "tpdB", "tpcA", "mc56", "tPdA", "iqa", "tx3A", "iPdB", "tPcA", "tPdB", "tqa", "tx3B", "ix3A",
    "ix3B", "ipdB", "tx1A", "tx1B", "tPcB", "iPcA", "iPdA", "mp3", "sh3q", "mp2", "sh2q", "tqb", "sh3p",
    "sh1q", "tpdA", "mp0", "ix0B", "ix0A", "iqcA", "iqcB", "sh0q", "iqb", "sh2p", "mc0", "sh0p", "tqdA",
    "iyB", "iqdA", "tyA", "ipcB", "ipcA", "iyA", "tqcA", "tqdB", "iqdB", "tyB", "tqcB", "ioQA", "toPA",
    "toQA", "ioPB", "ioQB", "toPB", "toQB", "ioPA",
]


def peers():
    b, g = lax.axis_index("blk"), lax.axis_index("grp")
    xl, y = b // 4, lax.rem(b, 4)
    z, low = g // 4, lax.rem(g, 4)
    xh, core = low // 2, lax.rem(low, 2)

    def at(xl, y, z, xh, core):
        return (xl * 4 + y, z * 4 + xh * 2 + core)

    up = lambda v: lax.rem(v + 1, 4)
    down = lambda v: lax.rem(v + 3, 4)
    pictures = (at(xl, y, up(z), xh, core), at(xl, y, down(z), xh, core), at(1 - xl, y, z, xh, core))
    captions = (at(xl, up(y), z, xh, core), at(xl, down(y), z, xh, core), at(1 - xl, y, z, 1 - xh, core))
    sibling = at(xl, y, z, xh, 1 - core)
    starts = []
    for dy, dx in ORDER:
        txl = 1 - xl if dx else xl
        txh = 1 - xh if dx else xh
        blk, grp = at(txl, lax.rem(y + dy, 4), z, txh, core)
        starts.append((blk * 16 + grp) * SHARE)
    return pictures, captions, sibling, starts


class Family:
    def __init__(self, shares, step, sums, other, devices, out, first):
        self.shares, self.step, self.sums, self.other = shares, step, sums, other
        self.plus, self.minus, self.pair = devices
        self.out, self.first = out, first
        self.sent = {}

    def rows(self, key, lo, hi):
        return self.shares.at[pl.ds(SLOT[key] * self.step + lo, hi - lo)]


def kernel(
    sharp_ref, shift_ref, picture_ref, caption_ref, label_ref, picture_out, caption_out,
    pictures, captions, own_labels, labels, weights, picture_sums, caption_sums, sibling_sums,
    out_data, in_data, local_sem, send_sem, recv_sem,
):
    picture_peers, caption_peers, sibling, starts = peers()
    loads = [
        pltpu.make_async_copy(picture_ref, pictures.at[pl.ds(0, SHARE)], local_sem.at[0]),
        pltpu.make_async_copy(caption_ref, captions.at[pl.ds(0, SHARE)], local_sem.at[1]),
        pltpu.make_async_copy(label_ref, own_labels, local_sem.at[2]),
    ]
    for load in loads:
        load.start()
    barrier = pltpu.get_barrier_semaphore()
    everyone = [*picture_peers, *caption_peers, sibling]
    for device in everyone:
        pl.semaphore_signal(barrier, inc=1, device_id=device, device_id_type=MESH)
    half_sharp = sharp_ref[0] * 0.5
    half_shift = shift_ref[0] * 0.5
    for load in loads:
        load.wait()
    labels[0] = jnp.broadcast_to(own_labels[...], (8, SHARE))
    pl.semaphore_wait(barrier, len(everyone))

    width = picture_ref.shape[1]
    copies = []

    def send(src, dst, device):
        i = len(copies)
        copy = pltpu.make_async_remote_copy(
            src_ref=src, dst_ref=dst, send_sem=send_sem.at[i], recv_sem=recv_sem.at[i],
            device_id=device, device_id_type=MESH,
        )
        copy.start()
        copies.append(copy)
        return copy

    images = Family(pictures, 2 * SHARE, picture_sums, sibling_sums, picture_peers, picture_out, 0)
    texts = Family(captions, SHARE, caption_sums, None, caption_peers, caption_out, len(ROUTE))
    both = (images, texts)
    mid_p, mid_q = HALF // 2, HALF + HALF // 2

    def hop(f, name, key, lo, hi, to, device):
        f.sent[name] = send(f.rows(key, lo, hi), f.rows(to, lo, hi), device)

    def label_hop(name, key, to, device):
        images.sent[name] = send(labels.at[2 * SLOT[key]], labels.at[2 * SLOT[to]], device)

    def to_sibling(*keys):
        for key in keys:
            start = SLOT[key] * 2 * SHARE
            images.sent["s", key] = send(
                pictures.at[pl.ds(start, SHARE)], pictures.at[pl.ds(start + SHARE, SHARE)], sibling
            )
            images.sent["l", key] = send(labels.at[2 * SLOT[key]], labels.at[2 * SLOT[key] + 1], sibling)

    def arrive(f, *names):
        for name in names:
            f.sent[name].wait_recv()

    def from_sibling(*keys):
        for key in keys:
            arrive(images, ("s", key), ("l", key))

    def around(f, tag, key, to_plus, to_minus, lo):
        mid, hi = lo + HALF // 2, lo + HALF
        hop(f, tag + "+a", key, lo, mid, to_plus, f.plus)
        hop(f, tag + "-b", key, mid, hi, to_minus, f.minus)
        hop(f, tag + "+b", key, mid, hi, to_plus, f.plus)
        hop(f, tag + "-a", key, lo, mid, to_minus, f.minus)

    def onward(f, tag, dx, lo):
        arrive(f, tag + "+a", tag + "-b")
        hop(f, tag + "++", (3, dx), lo, lo + HALF // 2, (2, dx), f.plus)
        hop(f, tag + "--", (1, dx), lo + HALF // 2, lo + HALF, (2, dx), f.minus)

    to_sibling((0, 0))
    for f in both:
        around(f, "q", (0, 0), (3, 0), (1, 0), HALF)
        hop(f, "xp", (0, 0), 0, HALF, (0, 1), f.pair)
    label_hop("xl", (0, 0), (0, 1), images.pair)
    label_hop("l+", (0, 0), (3, 0), images.plus)
    label_hop("l-", (0, 0), (1, 0), images.minus)
    for f in both:
        around(f, "p", (0, 0), (3, 0), (1, 0), 0)
        hop(f, "xq", (0, 0), HALF, SHARE, (0, 1), f.pair)
    for f in both:
        onward(f, "q", 0, HALF)
    for f in both:
        arrive(f, "q+b", "q-a")
        hop(f, "xq1", (1, 0), HALF, SHARE, (1, 1), f.pair)
        hop(f, "xq3", (3, 0), HALF, SHARE, (3, 1), f.pair)
    arrive(images, "l+", "l-", "xl")
    label_hop("l++", (3, 0), (2, 0), images.plus)
    label_hop("L+", (0, 1), (3, 1), images.plus)
    label_hop("L-", (0, 1), (1, 1), images.minus)
    for f in both:
        onward(f, "p", 0, 0)
    for f in both:
        arrive(f, "xp")
        around(f, "P", (0, 1), (3, 1), (1, 1), 0)
    arrive(images, "p+b", "p-a")
    to_sibling((3, 0), (1, 0))
    arrive(images, "xq")
    to_sibling((0, 1))
    arrive(texts, "p+b", "p-a", "xq")
    arrive(images, "L+", "L-")
    label_hop("L++", (3, 1), (2, 1), images.plus)
    for f in both:
        arrive(f, "q++", "q--")
        hop(f, "xq2", (2, 0), HALF, SHARE, (2, 1), f.pair)

    def weigh(first_text, texts, first_image, images):
        @pl.loop(first_image, first_image + images)
        def _(ii):
            columns = pl.ds(pl.multiple_of(ii * 2 * SHARE, 2 * SHARE), 2 * SHARE)
            scores = lax.dot_general(
                captions[pl.ds(first_text * SHARE, texts * SHARE), :], pictures[columns, :],
                (((1,), (1,)), ((), ())), preferred_element_type=jnp.float32,
            )
            label = jnp.concatenate([labels[2 * ii, :1, :], labels[2 * ii + 1, :1, :]], axis=1)
            ids = lax.broadcasted_iota(jnp.int32, (SHARE, 2 * SHARE), 0)
            for j in range(texts):
                own = ids == label - starts[first_text + j]
                part = scores[j * SHARE : (j + 1) * SHARE] * half_sharp + half_shift
                twice = jnp.tanh(part) + jnp.where(own, -1.0, 1.0)
                weights[pl.ds((first_text + j) * SHARE, SHARE), columns] = twice.astype(jnp.bfloat16)

    def add(sums, rows, value, more):
        sums[rows, :] = sums[rows, :] + value if more else value

    def multiply_pictures(first, count, lo, hi, more=False):
        rows, inner = pl.ds(first * 2 * SHARE, count * 2 * SHARE), pl.ds(lo * SHARE, (hi - lo) * SHARE)
        value = lax.dot_general(
            weights[inner, rows], captions[inner, :], (((0,), (0,)), ((), ())), preferred_element_type=jnp.float32
        )
        add(picture_sums, rows, value, more)

    def multiply_captions(first, count, lo, hi, more=False):
        rows, inner = pl.ds(first * SHARE, count * SHARE), pl.ds(lo * 2 * SHARE, (hi - lo) * 2 * SHARE)
        value = jnp.dot(weights[rows, inner], pictures[inner, :], preferred_element_type=jnp.float32)
        add(caption_sums, rows, value, more)

    from_sibling((0, 0), (3, 0), (1, 0), (0, 1))
    for f in both:
        arrive(f, "p++", "p--")
    arrive(images, "l++")
    to_sibling((2, 0))
    weigh(0, EARLY, 0, 2)
    for f in both:
        onward(f, "P", 1, 0)
    weigh(0, EARLY, 2, 2)
    from_sibling((2, 0))
    weigh(0, EARLY, 4, 1)
    for f in both:
        arrive(f, "P+b", "P-a", "xq1", "xq3")
    to_sibling((3, 1), (1, 1))
    multiply_captions(0, EARLY, 0, EARLY)
    from_sibling((3, 1), (1, 1))
    arrive(images, "P++", "P--", "L++", "xq2")
    to_sibling((2, 1))
    weigh(0, EARLY, 5, 2)
    arrive(texts, "P++", "P--", "xq2")
    from_sibling((2, 1))

    def wide(tile):
        return jnp.concatenate([jnp.concatenate([tile] * (width // 128), axis=1)] * (UNIT // 8), axis=0)

    landed = set()

    def land(f, names):
        for name in names:
            if (f, name) not in landed:
                landed.add((f, name))
                for copy in f.sent[name]:
                    copy.wait_recv()

    def total(f, key, lo, names):
        x = f.sums[pl.ds(SLOT[key] * f.step + lo, UNIT), :]
        if f.other is not None:
            land(f, [f"sh{SLOT[key]}" + "pq"[lo // HALF]])
            x = x + f.other[SLOT[key], pl.ds(lo, UNIT), :]
        land(f, names)
        for name in names:
            index = f.first + NUMBER[name]
            rows = [jnp.concatenate([in_data[index, TILES * r + c] for c in range(TILES)], axis=1) for r in (0, 1)]
            power = in_data[index, 2 * TILES].astype(jnp.int32).astype(jnp.float32)
            scale = jnp.exp2(power[:8]) * (1.0 / TOP)
            x = x + jnp.concatenate(rows, axis=0).astype(jnp.int32).astype(jnp.float32) * wide(scale)
        return x

    def pass_on(f, name):
        key, lo, way, names = ROUTE[name]
        index = f.first + NUMBER[name]
        x = total(f, key, lo, names)
        size = jnp.abs(x)
        peak = jnp.full((8, 128), 1e-30, jnp.float32)
        for r in range(0, UNIT, 8):
            for c in range(0, width, 128):
                peak = jnp.maximum(peak, size[r : r + 8, c : c + 128])
        power = jnp.ceil(jnp.log2(peak))
        whole = jnp.round(x * wide(TOP * jnp.exp2(-power))).astype(jnp.int32).astype(jnp.int16)
        for r in (0, 1):
            for c in range(TILES):
                out_data[index, TILES * r + c] = whole[16 * r : 16 * r + 16, 128 * c : 128 * c + 128]
        out_data[index, 2 * TILES] = jnp.concatenate([power, power], axis=0).astype(jnp.int32).astype(jnp.int16)
        f.sent[name] = (send(out_data.at[index], in_data.at[index], getattr(f, way)),)

    drained = [0]

    def drain(keep):
        while drained[0] < len(copies) - keep:
            copies[drained[0]].wait_send()
            drained[0] += 1

    def work(name):
        slots = [int(digit) for digit in name[2:] if digit.isdigit()]
        if name == "W7":
            weigh(0, EARLY, 7, 1)
        elif name[0] == "V":
            weigh(EARLY, 8 - EARLY, int(name[1]), 1)
        elif name[:2] in ("mp", "mc"):
            multiply = multiply_pictures if name[1] == "p" else multiply_captions
            begun = name[1] == "c" and min(slots) < EARLY
            multiply(min(slots), len(slots), EARLY if begun else 0, 8, begun)
        elif name[:2] == "sh":
            i = slots[0]
            at = HALF if name[-1] == "q" else 0
            rows = pl.ds(i * 2 * SHARE + SHARE + at, HALF)
            images.sent[name] = (send(picture_sums.at[rows], sibling_sums.at[i, pl.ds(at, HALF)], sibling),)
        else:
            f = images if name[0] == "i" else texts
            if name[1:] in ROUTE:
                pass_on(f, name[1:])
            else:
                lo, names = RESULT[name[1:]]
                drain(24)
                f.out[pl.ds(lo, UNIT), :] = total(f, (0, 0), lo, names)

    for name in PLAN:
        work(name)
    drain(0)


COPIES = 46 + 16 + 7 + 16 + 2 * len(ROUTE)


def per_device(picture_vectors, caption_vectors, matching_caption, sharpness_parameter, additive_intercept):
    width = picture_vectors.shape[1]
    f32, bf16 = jnp.float32, jnp.bfloat16
    out = jax.ShapeDtypeStruct((SHARE, width), f32)
    vmem, smem = pl.BlockSpec(memory_space=pltpu.VMEM), pl.BlockSpec(memory_space=pltpu.SMEM)
    anywhere = pl.BlockSpec(memory_space=pltpu.HBM)
    arrays = [
        pltpu.with_memory_space_constraint(array, pltpu.HBM)
        for array in (picture_vectors, caption_vectors, matching_caption[None, :])
    ]
    picture_sums, caption_sums = pl.pallas_call(
        kernel,
        out_shape=(out, out),
        in_specs=[smem, smem, anywhere, anywhere, anywhere],
        out_specs=(vmem, vmem),
        scratch_shapes=[
            pltpu.VMEM((16 * SHARE, width), bf16),
            pltpu.VMEM((8 * SHARE, width), bf16),
            pltpu.VMEM((1, SHARE), jnp.int32),
            pltpu.VMEM((16, 8, SHARE), jnp.int32),
            pltpu.VMEM((8 * SHARE, 16 * SHARE), bf16),
            pltpu.VMEM((16 * SHARE, width), f32),
            pltpu.VMEM((8 * SHARE, width), f32),
            pltpu.VMEM((8, SHARE, width), f32),
            pltpu.VMEM((2 * len(ROUTE), 2 * TILES + 1, 16, 128), jnp.int16),
            pltpu.VMEM((2 * len(ROUTE), 2 * TILES + 1, 16, 128), jnp.int16),
            pltpu.SemaphoreType.DMA((3,)),
            pltpu.SemaphoreType.DMA((COPIES,)),
            pltpu.SemaphoreType.DMA((COPIES,)),
        ],
        compiler_params=pltpu.CompilerParams(
            collective_id=0, has_side_effects=True, vmem_limit_bytes=46 * 2**20
        ),
        cost_estimate=pl.CostEstimate(
            flops=6 * 2048 * 1024 * width, bytes_accessed=6 * SHARE * width * 2, transcendentals=2048 * 1024
        ),
        name="pair_loss_backward",
    )(sharpness_parameter, additive_intercept, *arrays)
    scale = 0.5 * sharpness_parameter[0]
    return scale * picture_sums, scale * caption_sums


def solution(mesh):
    placed = (P(("blk", "grp"), None), P(("blk", "grp"), None), P(("blk", "grp")), P(), P())
    return jax.shard_map(
        per_device,
        mesh=mesh,
        in_specs=placed,
        out_specs=(P(("blk", "grp"), None), P(("blk", "grp"), None)),
        check_vma=False,
    )
```

```python
import functools

import jax
import jax.numpy as jnp
from jax import lax
from jax.experimental import pallas as pl
from jax.experimental.pallas import tpu as pltpu
from jax.sharding import PartitionSpec as P

MESH = pl.DeviceIdType.MESH
ORDER = [(0, 0), (3, 0), (1, 0), (0, 1), (2, 0), (3, 1), (1, 1), (2, 1)]
SLOT = {key: i for i, key in enumerate(ORDER)}
EARLY = 5
SHARE = 128
HALF = 64
UNIT = 32
TILES = 9
TOP = 32760.0

ROUTE = {}
RESULT = {}
for part, at in (("A", 0), ("B", UNIT)):
    for step in range(4):
        ROUTE[f"x{step}{part}"] = ((step, 1), HALF + at, "pair", ())
    ROUTE["y" + part] = ((0, 1), at, "pair", ("Pc" + part, "Pd" + part))
    RESULT["oP" + part] = (at, ("pc" + part, "pd" + part, "y" + part))
    RESULT["oQ" + part] = (HALF + at, ("qc" + part, "qd" + part, "x0" + part))
    for tag, dx, low in (("P", 1, 0), ("p", 0, 0), ("q", 0, HALF)):
        came = lambda step: (f"x{step}{part}",) if tag == "q" else ()
        far, way = ("a", "plus") if part == "A" else ("b", "minus")
        ROUTE[tag + far] = ((2, dx), low + at, way, came(2))
        ROUTE[tag + "c" + part] = ((1, dx), low + at, "plus", came(1) + ((tag + "a",) if part == "A" else ()))
        ROUTE[tag + "d" + part] = ((3, dx), low + at, "minus", came(3) + ((tag + "b",) if part == "B" else ()))
NUMBER = {name: i for i, name in enumerate(ROUTE)}

PLAN = [
    "V4", "V1", "W7", "V0", "V6", "V3", "V7", "mp76", "sh7q", "sh7p", "sh6p", "sh6q", "mc34", "tx0B", "tpa",
    "mp1", "iPb", "iPa", "ix2B", "sh1p", "ix2A", "mp4", "sh4p", "iPcB", "ix1B", "sh4q", "tx0A", "tpb", "V2",
    "ipdA", "V5", "ipa", "mc7", "tPa", "tx2A", "tPb", "ipb", "mp5", "sh5q", "tx2B", "ix1A", "sh5p", "mc12",
    "tpcB", "tpdB", "tpcA", "mc56", "tPdA", "iqa", "tx3A", "iPdB", "tPcA", "tPdB", "tqa", "tx3B", "ix3A",
    "ix3B", "ipdB", "tx1A", "tx1B", "tPcB", "iPcA", "iPdA", "mp3", "sh3q", "mp2", "sh2q", "tqb", "sh3p",
    "sh1q", "tpdA", "mp0", "ix0B", "ix0A", "iqcA", "iqcB", "sh0q", "iqb", "sh2p", "mc0", "sh0p", "tqdA",
    "iyB", "iqdA", "tyA", "ipcB", "ipcA", "iyA", "tqcA", "tqdB", "iqdB", "tyB", "tqcB", "ioQA", "toPA",
    "toQA", "ioPB", "ioQB", "toPB", "toQB", "ioPA",
]


def peers():
    b, g = lax.axis_index("blk"), lax.axis_index("grp")
    xl, y = b // 4, lax.rem(b, 4)
    z, low = g // 4, lax.rem(g, 4)
    xh, core = low // 2, lax.rem(low, 2)

    def at(xl, y, z, xh, core):
        return (xl * 4 + y, z * 4 + xh * 2 + core)

    up = lambda v: lax.rem(v + 1, 4)
    down = lambda v: lax.rem(v + 3, 4)
    pictures = (at(xl, y, up(z), xh, core), at(xl, y, down(z), xh, core), at(1 - xl, y, z, xh, core))
    captions = (at(xl, up(y), z, xh, core), at(xl, down(y), z, xh, core), at(1 - xl, y, z, 1 - xh, core))
    sibling = at(xl, y, z, xh, 1 - core)
    starts = []
    for dy, dx in ORDER:
        txl = 1 - xl if dx else xl
        txh = 1 - xh if dx else xh
        blk, grp = at(txl, lax.rem(y + dy, 4), z, txh, core)
        starts.append((blk * 16 + grp) * SHARE)
    return pictures, captions, sibling, starts


class Family:
    def __init__(self, shares, step, sums, other, devices, out, first):
        self.shares, self.step, self.sums, self.other = shares, step, sums, other
        self.plus, self.minus, self.pair = devices
        self.out, self.first = out, first
        self.sent = {}

    def rows(self, key, lo, hi):
        return self.shares.at[pl.ds(SLOT[key] * self.step + lo, hi - lo)]


def kernel(
    sharp_ref, shift_ref, picture_ref, caption_ref, label_ref, picture_out, caption_out,
    pictures, captions, own_labels, labels, weights, picture_sums, caption_sums, sibling_sums,
    out_data, in_data, local_sem, send_sem, recv_sem,
):
    picture_peers, caption_peers, sibling, starts = peers()
    loads = [
        pltpu.make_async_copy(picture_ref, pictures.at[pl.ds(0, SHARE)], local_sem.at[0]),
        pltpu.make_async_copy(caption_ref, captions.at[pl.ds(0, SHARE)], local_sem.at[1]),
        pltpu.make_async_copy(label_ref, own_labels, local_sem.at[2]),
    ]
    for load in loads:
        load.start()
    barrier = pltpu.get_barrier_semaphore()
    everyone = [*picture_peers, *caption_peers, sibling]
    for device in everyone:
        pl.semaphore_signal(barrier, inc=1, device_id=device, device_id_type=MESH)
    half_sharp = sharp_ref[0] * 0.5
    half_shift = shift_ref[0] * 0.5
    for load in loads:
        load.wait()
    labels[0] = jnp.broadcast_to(own_labels[...], (8, SHARE))
    pl.semaphore_wait(barrier, len(everyone))

    width = picture_ref.shape[1]
    copies = []

    def send(src, dst, device):
        i = len(copies)
        copy = pltpu.make_async_remote_copy(
            src_ref=src, dst_ref=dst, send_sem=send_sem.at[i], recv_sem=recv_sem.at[i],
            device_id=device, device_id_type=MESH,
        )
        copy.start()
        copies.append(copy)
        return copy

    images = Family(pictures, 2 * SHARE, picture_sums, sibling_sums, picture_peers, picture_out, 0)
    texts = Family(captions, SHARE, caption_sums, None, caption_peers, caption_out, len(ROUTE))
    both = (images, texts)
    mid_p, mid_q = HALF // 2, HALF + HALF // 2

    def hop(f, name, key, lo, hi, to, device):
        f.sent[name] = send(f.rows(key, lo, hi), f.rows(to, lo, hi), device)

    def label_hop(name, key, to, device):
        images.sent[name] = send(labels.at[2 * SLOT[key]], labels.at[2 * SLOT[to]], device)

    def to_sibling(*keys):
        for key in keys:
            start = SLOT[key] * 2 * SHARE
            images.sent["s", key] = send(
                pictures.at[pl.ds(start, SHARE)], pictures.at[pl.ds(start + SHARE, SHARE)], sibling
            )
            images.sent["l", key] = send(labels.at[2 * SLOT[key]], labels.at[2 * SLOT[key] + 1], sibling)

    def arrive(f, *names):
        for name in names:
            f.sent[name].wait_recv()

    def from_sibling(*keys):
        for key in keys:
            arrive(images, ("s", key), ("l", key))

    def around(f, tag, key, to_plus, to_minus, lo):
        mid, hi = lo + HALF // 2, lo + HALF
        hop(f, tag + "+a", key, lo, mid, to_plus, f.plus)
        hop(f, tag + "-b", key, mid, hi, to_minus, f.minus)
        hop(f, tag + "+b", key, mid, hi, to_plus, f.plus)
        hop(f, tag + "-a", key, lo, mid, to_minus, f.minus)

    def onward(f, tag, dx, lo):
        arrive(f, tag + "+a", tag + "-b")
        hop(f, tag + "++", (3, dx), lo, lo + HALF // 2, (2, dx), f.plus)
        hop(f, tag + "--", (1, dx), lo + HALF // 2, lo + HALF, (2, dx), f.minus)

    to_sibling((0, 0))
    for f in both:
        around(f, "q", (0, 0), (3, 0), (1, 0), HALF)
        hop(f, "xp", (0, 0), 0, HALF, (0, 1), f.pair)
    label_hop("xl", (0, 0), (0, 1), images.pair)
    label_hop("l+", (0, 0), (3, 0), images.plus)
    label_hop("l-", (0, 0), (1, 0), images.minus)
    for f in both:
        around(f, "p", (0, 0), (3, 0), (1, 0), 0)
        hop(f, "xq", (0, 0), HALF, SHARE, (0, 1), f.pair)
    for f in both:
        onward(f, "q", 0, HALF)
    for f in both:
        arrive(f, "q+b", "q-a")
        hop(f, "xq1", (1, 0), HALF, SHARE, (1, 1), f.pair)
        hop(f, "xq3", (3, 0), HALF, SHARE, (3, 1), f.pair)
    arrive(images, "l+", "l-", "xl")
    label_hop("l++", (3, 0), (2, 0), images.plus)
    label_hop("L+", (0, 1), (3, 1), images.plus)
    label_hop("L-", (0, 1), (1, 1), images.minus)
    for f in both:
        onward(f, "p", 0, 0)
    for f in both:
        arrive(f, "xp")
        around(f, "P", (0, 1), (3, 1), (1, 1), 0)
    arrive(images, "p+b", "p-a")
    to_sibling((3, 0), (1, 0))
    arrive(images, "xq")
    to_sibling((0, 1))
    arrive(texts, "p+b", "p-a", "xq")
    arrive(images, "L+", "L-")
    label_hop("L++", (3, 1), (2, 1), images.plus)
    for f in both:
        arrive(f, "q++", "q--")
        hop(f, "xq2", (2, 0), HALF, SHARE, (2, 1), f.pair)

    def weigh(first_text, texts, first_image, images):
        @pl.loop(first_image, first_image + images)
        def _(ii):
            columns = pl.ds(pl.multiple_of(ii * 2 * SHARE, 2 * SHARE), 2 * SHARE)
            scores = lax.dot_general(
                captions[pl.ds(first_text * SHARE, texts * SHARE), :], pictures[columns, :],
                (((1,), (1,)), ((), ())), preferred_element_type=jnp.float32,
            )
            label = jnp.concatenate([labels[2 * ii, :1, :], labels[2 * ii + 1, :1, :]], axis=1)
            ids = lax.broadcasted_iota(jnp.int32, (SHARE, 2 * SHARE), 0)
            for j in range(texts):
                own = ids == label - starts[first_text + j]
                part = scores[j * SHARE : (j + 1) * SHARE] * half_sharp + half_shift
                twice = jnp.tanh(part) + jnp.where(own, -1.0, 1.0)
                weights[pl.ds((first_text + j) * SHARE, SHARE), columns] = twice.astype(jnp.bfloat16)

    def add(sums, rows, value, more):
        sums[rows, :] = sums[rows, :] + value if more else value

    def multiply_pictures(first, count, lo, hi, more=False):
        rows, inner = pl.ds(first * 2 * SHARE, count * 2 * SHARE), pl.ds(lo * SHARE, (hi - lo) * SHARE)
        value = lax.dot_general(
            weights[inner, rows], captions[inner, :], (((0,), (0,)), ((), ())), preferred_element_type=jnp.float32
        )
        add(picture_sums, rows, value, more)

    def multiply_captions(first, count, lo, hi, more=False):
        rows, inner = pl.ds(first * SHARE, count * SHARE), pl.ds(lo * 2 * SHARE, (hi - lo) * 2 * SHARE)
        value = jnp.dot(weights[rows, inner], pictures[inner, :], preferred_element_type=jnp.float32)
        add(caption_sums, rows, value, more)

    from_sibling((0, 0), (3, 0), (1, 0), (0, 1))
    for f in both:
        arrive(f, "p++", "p--")
    arrive(images, "l++")
    to_sibling((2, 0))
    weigh(0, EARLY, 0, 2)
    for f in both:
        onward(f, "P", 1, 0)
    weigh(0, EARLY, 2, 2)
    from_sibling((2, 0))
    weigh(0, EARLY, 4, 1)
    for f in both:
        arrive(f, "P+b", "P-a", "xq1", "xq3")
    to_sibling((3, 1), (1, 1))
    multiply_captions(0, EARLY, 0, EARLY)
    from_sibling((3, 1), (1, 1))
    arrive(images, "P++", "P--", "L++", "xq2")
    to_sibling((2, 1))
    weigh(0, EARLY, 5, 2)
    arrive(texts, "P++", "P--", "xq2")
    from_sibling((2, 1))

    def wide(tile):
        return jnp.concatenate([jnp.concatenate([tile] * (width // 128), axis=1)] * (UNIT // 8), axis=0)

    landed = set()

    def land(f, names):
        for name in names:
            if (f, name) not in landed:
                landed.add((f, name))
                for copy in f.sent[name]:
                    copy.wait_recv()

    def total(f, key, lo, names):
        x = f.sums[pl.ds(SLOT[key] * f.step + lo, UNIT), :]
        if f.other is not None:
            land(f, [f"sh{SLOT[key]}" + "pq"[lo // HALF]])
            x = x + f.other[SLOT[key], pl.ds(lo, UNIT), :]
        land(f, names)
        for name in names:
            index = f.first + NUMBER[name]
            rows = [jnp.concatenate([in_data[index, TILES * r + c] for c in range(TILES)], axis=1) for r in (0, 1)]
            power = in_data[index, 2 * TILES].astype(jnp.int32).astype(jnp.float32)
            scale = jnp.exp2(power[:8]) * (1.0 / TOP)
            x = x + jnp.concatenate(rows, axis=0).astype(jnp.int32).astype(jnp.float32) * wide(scale)
        return x

    drained = [0]

    def drain(keep):
        while drained[0] < len(copies) - keep:
            copies[drained[0]].wait_send()
            drained[0] += 1

    def pass_on(f, name):
        key, lo, way, names = ROUTE[name]
        if name[0] == "y":
            drain(40)
        index = f.first + NUMBER[name]
        x = total(f, key, lo, names)
        size = jnp.abs(x)
        peak = jnp.full((8, 128), 1e-30, jnp.float32)
        for r in range(0, UNIT, 8):
            for c in range(0, width, 128):
                peak = jnp.maximum(peak, size[r : r + 8, c : c + 128])
        power = jnp.ceil(jnp.log2(peak))
        whole = jnp.round(x * wide(TOP * jnp.exp2(-power))).astype(jnp.int32).astype(jnp.int16)
        for r in (0, 1):
            for c in range(TILES):
                out_data[index, TILES * r + c] = whole[16 * r : 16 * r + 16, 128 * c : 128 * c + 128]
        out_data[index, 2 * TILES] = jnp.concatenate([power, power], axis=0).astype(jnp.int32).astype(jnp.int16)
        f.sent[name] = (send(out_data.at[index], in_data.at[index], getattr(f, way)),)

    def work(name):
        slots = [int(digit) for digit in name[2:] if digit.isdigit()]
        if name == "W7":
            weigh(0, EARLY, 7, 1)
        elif name[0] == "V":
            weigh(EARLY, 8 - EARLY, int(name[1]), 1)
        elif name[:2] in ("mp", "mc"):
            multiply = multiply_pictures if name[1] == "p" else multiply_captions
            begun = name[1] == "c" and min(slots) < EARLY
            multiply(min(slots), len(slots), EARLY if begun else 0, 8, begun)
        elif name[:2] == "sh":
            i = slots[0]
            at = HALF if name[-1] == "q" else 0
            rows = pl.ds(i * 2 * SHARE + SHARE + at, HALF)
            images.sent[name] = (send(picture_sums.at[rows], sibling_sums.at[i, pl.ds(at, HALF)], sibling),)
        else:
            f = images if name[0] == "i" else texts
            if name[1:] in ROUTE:
                pass_on(f, name[1:])
            else:
                lo, names = RESULT[name[1:]]
                drain(24)
                f.out[pl.ds(lo, UNIT), :] = total(f, (0, 0), lo, names)

    for name in PLAN:
        work(name)
    drain(0)


COPIES = 46 + 16 + 7 + 16 + 2 * len(ROUTE)


def per_device(picture_vectors, caption_vectors, matching_caption, sharpness_parameter, additive_intercept):
    width = picture_vectors.shape[1]
    f32, bf16 = jnp.float32, jnp.bfloat16
    out = jax.ShapeDtypeStruct((SHARE, width), f32)
    vmem, smem = pl.BlockSpec(memory_space=pltpu.VMEM), pl.BlockSpec(memory_space=pltpu.SMEM)
    anywhere = pl.BlockSpec(memory_space=pltpu.HBM)
    arrays = [
        pltpu.with_memory_space_constraint(array, pltpu.HBM)
        for array in (picture_vectors, caption_vectors, matching_caption[None, :])
    ]
    picture_sums, caption_sums = pl.pallas_call(
        kernel,
        out_shape=(out, out),
        in_specs=[smem, smem, anywhere, anywhere, anywhere],
        out_specs=(vmem, vmem),
        scratch_shapes=[
            pltpu.VMEM((16 * SHARE, width), bf16),
            pltpu.VMEM((8 * SHARE, width), bf16),
            pltpu.VMEM((1, SHARE), jnp.int32),
            pltpu.VMEM((16, 8, SHARE), jnp.int32),
            pltpu.VMEM((8 * SHARE, 16 * SHARE), bf16),
            pltpu.VMEM((16 * SHARE, width), f32),
            pltpu.VMEM((8 * SHARE, width), f32),
            pltpu.VMEM((8, SHARE, width), f32),
            pltpu.VMEM((2 * len(ROUTE), 2 * TILES + 1, 16, 128), jnp.int16),
            pltpu.VMEM((2 * len(ROUTE), 2 * TILES + 1, 16, 128), jnp.int16),
            pltpu.SemaphoreType.DMA((3,)),
            pltpu.SemaphoreType.DMA((COPIES,)),
            pltpu.SemaphoreType.DMA((COPIES,)),
        ],
        compiler_params=pltpu.CompilerParams(
            collective_id=0, has_side_effects=True, vmem_limit_bytes=46 * 2**20
        ),
        cost_estimate=pl.CostEstimate(
            flops=6 * 2048 * 1024 * width, bytes_accessed=6 * SHARE * width * 2, transcendentals=2048 * 1024
        ),
        name="pair_loss_backward",
    )(sharpness_parameter, additive_intercept, *arrays)
    scale = 0.5 * sharpness_parameter[0]
    return scale * picture_sums, scale * caption_sums


def solution(mesh):
    placed = (P(("blk", "grp"), None), P(("blk", "grp"), None), P(("blk", "grp")), P(), P())
    return jax.shard_map(
        per_device,
        mesh=mesh,
        in_specs=placed,
        out_specs=(P(("blk", "grp"), None), P(("blk", "grp"), None)),
        check_vma=False,
    )
```
